512 devices in a mesh: row: 64 (over x, z), col: 8 (over y, core).
Axes of the slice: x: 4, y: 4, z: 16, core: 2. Of those that a mesh axis runs over, the one named last changes fastest.
Arguments:
- omega_tiles: float32 [512, 24, 128, 128], P('row', 'col'), may hold values from -0.3 to 0.3
- omega_diag: float32 [65536, 128], P(('row', 'col')), may hold values from -0.25 to 2, as said below
- samples: float32 [65536, 128], P(('row', 'col')), may hold values from -6 to 6
- pattern: int32 [512, 24], P('row', 'col'), may hold values from 0 to 511, as said below
Outputs:
- next_tiles: float32 [512, 24, 128, 128], P('row', 'col')
- next_diag: float32 [65536, 128], P(('row', 'col'))
The draws below stay inside these ranges and needn't reach their ends.
Inputs may be any that keep to these rules, and one draw needn't show every extreme that they name: `pattern`: block j stands at slot s of block row i exactly when block i stands at slot s of block row j, and never in the same group of 8 block rows as i. For the block rows of one index of row and the 3 slots of one index of col, at most 1 listed blocks fall in the block rows of any one other index of row, and exactly 1 for some. A block may stand at more than one slot of a row. `omega_diag`: each row's entry on the diagonal of its block lies in 1 to 2; the others lie within -0.25 to 0.25.
All inputs are finite; a program needn't handle non-finite values.
Results may differ from the reference program's by a relative error of at most 0.00012.
Values sent between devices are 32-bit elements; how exact they have to be, the bound alone decides.
No kernel may reach another device: no remote copies, remote signals or barrier semaphores. Data moves between devices by JAX's collectives and lax.ppermute only.
A program may use at most 64 MiB of HBM per device.

```python
import jax
import jax.numpy as jnp
import numpy as np
from jax import lax

BS = 128
K = 24
BR_DEV = 8
NS = 128
ITERS = 2
NB = 512
P_SIZE = 65536
N_ROW = 64
N_COL = 8


def draw_samples(key, part):
    key_one = jax.random.fold_in(jax.random.fold_in(key, 11), 0)
    result = jnp.clip(jax.random.normal(key_one, (P_SIZE, NS), jnp.float32), -6.0, 6.0)
    return result.astype(jnp.float32)


def draw_omega_diag(key, part):
    key_one, key_two = jax.random.split(jax.random.fold_in(key, 3))
    spread = jnp.clip(0.05 * jax.random.normal(key_one, (P_SIZE, BS), jnp.float32), -0.25, 0.25)
    pivots = jax.random.uniform(key_two, (P_SIZE, 1), jnp.float32, 1.0, 2.0)
    column_pos = jnp.arange(BS, dtype=jnp.int32)[None, :]
    row_pos = (jnp.arange(P_SIZE, dtype=jnp.int32) % BS)[:, None]
    return jnp.where(column_pos == row_pos, pivots, spread).astype(jnp.float32)


def draw_pattern(key, part):
    slot_count = K // N_COL
    peer_span = N_ROW // 2 - 2
    unit_idx = np.zeros((N_COL, slot_count, BR_DEV), np.int32)
    signs = np.zeros((N_COL, slot_count, BR_DEV), np.int32)
    kinds = np.zeros((N_COL, slot_count, BR_DEV), np.int32)
    local_rows = np.zeros((N_COL, slot_count, BR_DEV), np.int32)
    col_table = np.zeros((N_COL, slot_count, BR_DEV), np.int32)
    leader_ids = {}
    for slot_index in range(slot_count):
        offset = 1 + slot_index % (BR_DEV - 1)
        for member in range(BR_DEV):
            partner = member ^ offset
            if slot_index == 0 and member < 2:
                continue
            leader = min(member, partner)
            if (slot_index, leader) not in leader_ids:
                leader_ids[slot_index, leader] = len(leader_ids)
    units = max(1, len(leader_ids))
    for col_index in range(N_COL):
        for slot_index in range(slot_count):
            offset = 1 + slot_index % (BR_DEV - 1)
            for member in range(BR_DEV):
                partner = member ^ offset
                col_table[col_index, slot_index, member] = col_index
                if slot_index == 0 and member < 2:
                    kinds[col_index, slot_index, member] = 1 + member
                    local_rows[col_index, slot_index, member] = member
                    signs[col_index, slot_index, member] = 1
                else:
                    unit_idx[col_index, slot_index, member] = leader_ids[slot_index, min(member, partner)]
                    signs[col_index, slot_index, member] = 1 if member < partner else -1
                    local_rows[col_index, slot_index, member] = partner
    key_one, key_two = jax.random.split(jax.random.fold_in(key, 7))
    distances = jax.random.permutation(key_one, peer_span).astype(jnp.int32) + 2
    ordering = jax.random.permutation(key_two, units).astype(jnp.int32)
    position = (ordering[jnp.asarray(unit_idx)] + jnp.asarray(col_table)) % peer_span
    paired = (jnp.asarray(signs) * distances[position])[None]
    device_rows = jnp.arange(N_ROW, dtype=jnp.int32)[:, None, None, None]
    neighbour = jnp.where(device_rows % 2 == 0, 1, -1).astype(jnp.int32)
    kind_grid = jnp.asarray(kinds)[None]
    offsets = jnp.where(kind_grid == 0, paired, jnp.where(kind_grid == 1, N_ROW // 2, neighbour))
    target = (device_rows + offsets + N_ROW) % N_ROW * BR_DEV + jnp.asarray(local_rows)[None]
    return jnp.transpose(target, (0, 3, 1, 2)).reshape(N_ROW * BR_DEV, K).astype(jnp.int32)


def block_scale(key, shape, shards, smallest, largest):
    loudness = 1.0
    for axis_at, blocks in shards:
        steps = jax.random.uniform(jax.random.fold_in(jax.random.fold_in(key, 6), axis_at), (blocks,), jnp.float32, smallest / len(shards), largest / len(shards))
        loudness = loudness * jnp.repeat(jnp.exp(steps), shape[axis_at] // blocks).reshape((-1,) + (1,) * (len(shape) - 1 - axis_at))
    return loudness


def scatter_about(key, extent, deviation, bound, cuts=(), held_as=jnp.bfloat16):
    array = deviation * jax.random.normal(key, extent, jnp.float32)
    if cuts:
        array = array * block_scale(key, extent, cuts, -0.22, 0.18)
    return jnp.clip(array, -bound, bound).astype(held_as)


def setup_inputs(seed: int = 0) -> dict:
    key_list = jax.random.split(jax.random.key(seed), 5)
    omega_tiles = scatter_about(key_list[0], (NB, K, BS, BS), 0.05, 0.3, ((0, 64), (1, 8)), jnp.float32)
    omega_diag = draw_omega_diag(jax.random.fold_in(key_list[4], 71), 0)
    samples = draw_samples(jax.random.fold_in(key_list[4], 71), 0)
    pattern = draw_pattern(jax.random.fold_in(key_list[4], 71), 0)
    return dict(omega_tiles=omega_tiles, omega_diag=omega_diag, samples=samples, pattern=pattern)


step_size = 0.2
shrink_weight = 0.05
ridge_weight = 0.1


def soft_shrink(values, threshold):
    return values - jnp.clip(values, -threshold, threshold)


def reference(omega_tiles, omega_diag, samples, pattern):
    highest = lax.Precision.HIGHEST
    x_blocks = samples.reshape(NB, BS, NS)
    x_tiles = x_blocks[pattern]
    slot_ids = jnp.arange(K, dtype=jnp.int32)[None, :]
    identity = jnp.eye(BS, dtype=jnp.float32)
    tile_vals = omega_tiles
    diag_vals = omega_diag.reshape(NB, BS, BS)
    for sweep_index in range(ITERS):
        products = jnp.einsum("ikm,imn->ikn", diag_vals, x_blocks, precision=highest)
        products = products + jnp.einsum("iskm,ismn->ikn", tile_vals, x_tiles, precision=highest)
        cross_terms = jnp.einsum("ikn,isqn->iskq", products, x_tiles, precision=highest)
        mirror = jnp.swapaxes(cross_terms[pattern, slot_ids], 2, 3)
        gradient = (cross_terms + mirror) * (0.5 / NS) + ridge_weight * tile_vals
        tile_vals = soft_shrink(tile_vals - step_size * gradient, step_size * shrink_weight)
        self_cross = jnp.einsum("ikn,iqn->ikq", products, x_blocks, precision=highest)
        pivots = jnp.diagonal(diag_vals, axis1=1, axis2=2)
        diag_grad = (self_cross + jnp.swapaxes(self_cross, 1, 2)) * (0.5 / NS) + ridge_weight * diag_vals
        diag_grad = diag_grad - identity * (1.0 / pivots)[:, :, None]
        stepped = diag_vals - step_size * diag_grad
        diag_vals = identity * stepped + (1.0 - identity) * soft_shrink(stepped, step_size * shrink_weight)
    return tile_vals, diag_vals.reshape(P_SIZE, BS)
```

```python
import jax
import jax.numpy as jnp
from jax import lax
from jax.experimental import pallas as pl
from jax.experimental.pallas import tpu as pltpu
from jax.sharding import Mesh
from jax.sharding import PartitionSpec as P

ITERS = 2
STEP = 0.2
SHRINK = 0.05
RIDGE = 0.1

BS = 128
ROWS = 8
SLOTS = 3
TILES = ROWS * SLOTS
WANT = TILES + ROWS

X, Z, Y, CORE = 4, 16, 4, 2
ZL = 2
ZH = Z // ZL
COL = ("y", "k")
PEERS = ("x", "zl", "y", "k")
NP = X * ZL * Y * CORE
Q = BS // NP
GROUPS = NP // ROWS
TABLE = ZH * NP

VMEM = 48 * 1024 * 1024


def split(v):
    hi = v.astype(jnp.bfloat16)
    lo = (v - hi.astype(jnp.float32)).astype(jnp.bfloat16)
    return hi, lo


def dot(a, b, rhs_dim):
    return lax.dot_general(
        a, b, (((1,), (rhs_dim,)), ((), ())), preferred_element_type=jnp.float32
    )


def dot3(a, b, rhs_dim):
    return dot(a[0], b[0], rhs_dim) + (dot(a[0], b[1], rhs_dim) + dot(a[1], b[0], rhs_dim))


def shrink(v):
    t = STEP * SHRINK
    return v - jnp.clip(v, -t, t)


def select_kernel(idx, table, out, *, dests):
    first = pl.program_id(0) * dests

    def one(d, carry):
        base = (first + d) * WANT
        for t in range(WANT):
            out[d, t] = table[idx[base + t]]
        return carry

    lax.fori_loop(0, dests, one, 0)


def select(idx, table):
    dests = 8
    return pl.pallas_call(
        lambda i, t, o: select_kernel(i, t, o, dests=dests),
        grid_spec=pltpu.PrefetchScalarGridSpec(
            num_scalar_prefetch=1,
            grid=(NP // dests,),
            in_specs=[pl.BlockSpec((TABLE, Q, BS), lambda g, i: (0, 0, 0))],
            out_specs=pl.BlockSpec((dests, WANT, Q, BS), lambda g, i: (g, 0, 0, 0)),
        ),
        out_shape=jax.ShapeDtypeStruct((NP, WANT, Q, BS), jnp.float32),
        compiler_params=pltpu.CompilerParams(vmem_limit_bytes=VMEM),
    )(idx, table)


def assembled(recv, t):
    parts = [recv[pl.ds(t * Q + q, NP, stride=WANT * Q), :] for q in range(Q)]
    return jnp.concatenate(parts, axis=0)


def spread(out, i, value):
    for q in range(Q):
        out[pl.ds(i * Q + q, NP, stride=ROWS * Q), :] = value[q * NP : (q + 1) * NP]


def stacked(pairs, axis):
    return tuple(jnp.concatenate([p[n] for p in pairs], axis=axis) for n in range(2))


def first_kernel(col, recv, tiles, diag, xj, xi, sums):
    i = pl.program_id(0)
    xs = []
    for s in range(SLOTS):
        x = split(assembled(recv, i * SLOTS + s))
        xs.append(x)
        xj[0, s], xj[1, s] = x
    own = split(assembled(recv, TILES + i))
    xi[0, 0], xi[1, 0] = own
    bs = [split(tiles[0, s]) for s in range(SLOTS)]
    total = dot3(stacked(bs, 1), stacked(xs, 0), 0)
    spread(sums, i, total)

    @pl.when(i == col[0])
    def _():
        spread(sums, i, total + dot3(split(diag[...]), own, 0))


def sweep_kernel(col, recv, tiles, diag, xj, xi, new_tiles, new_diag, *rest):
    i = pl.program_id(0)
    own_x = (xi[0, 0], xi[1, 0])
    own_y = split(assembled(recv, TILES + i))
    lhs = stacked([own_y, own_x], 1)
    bs, xs = [], []
    for s in range(SLOTS):
        x = (xj[0, s], xj[1, s])
        y = split(assembled(recv, i * SLOTS + s))
        cross = dot3(lhs, stacked([x, y], 1), 1)
        old = tiles[0, s]
        new = shrink(old - STEP * (cross * (0.5 / BS) + RIDGE * old))
        new_tiles[0, s] = new
        if rest:
            bs.append(split(new))
            xs.append(x)
    if rest:
        total = dot3(stacked(bs, 1), stacked(xs, 0), 0)
        spread(rest[0], i, total)

    @pl.when(i == col[0])
    def _():
        cross = dot3(lhs, stacked([own_x, own_y], 1), 1)
        old = diag[...]
        shape = (BS, BS)
        eye = lax.broadcasted_iota(jnp.int32, shape, 0) == lax.broadcasted_iota(
            jnp.int32, shape, 1
        )
        pivots = jnp.where(eye, 1.0 / jnp.where(eye, old, 1.0), 0.0)
        stepped = old - STEP * (cross * (0.5 / BS) + RIDGE * old - pivots)
        new = jnp.where(eye, stepped, shrink(stepped))
        new_diag[...] = new
        if rest:
            spread(rest[0], i, total + dot3(split(new), own_x, 0))


whole_recv = pl.BlockSpec((NP * WANT * Q, BS), lambda i, c: (0, 0))
tile_spec = pl.BlockSpec((1, SLOTS, BS, BS), lambda i, c: (i, 0, 0, 0))
diag_spec = pl.BlockSpec((BS, BS), lambda i, c: (0, 0))
xj_spec = pl.BlockSpec((2, SLOTS, BS, BS), lambda i, c: (0, i, 0, 0))
xi_spec = pl.BlockSpec((2, 1, BS, BS), lambda i, c: (0, i, 0, 0))
sums_spec = pl.BlockSpec((NP * ROWS * Q, BS), lambda i, c: (0, 0))
xj_shape = jax.ShapeDtypeStruct((2, TILES, BS, BS), jnp.bfloat16)
xi_shape = jax.ShapeDtypeStruct((2, ROWS, BS, BS), jnp.bfloat16)
sums_shape = jax.ShapeDtypeStruct((NP * ROWS * Q, BS), jnp.float32)
tiles_shape = jax.ShapeDtypeStruct((ROWS, SLOTS, BS, BS), jnp.float32)
diag_shape = jax.ShapeDtypeStruct((BS, BS), jnp.float32)


def call(kernel, in_specs, out_specs, out_shape):
    return pl.pallas_call(
        kernel,
        grid_spec=pltpu.PrefetchScalarGridSpec(
            num_scalar_prefetch=1, grid=(ROWS,), in_specs=in_specs, out_specs=out_specs
        ),
        out_shape=out_shape,
        compiler_params=pltpu.CompilerParams(vmem_limit_bytes=VMEM),
    )


first_call = call(
    first_kernel,
    [whole_recv, tile_spec, diag_spec],
    [xj_spec, xi_spec, sums_spec],
    [xj_shape, xi_shape, sums_shape],
)
sweep_ins = [whole_recv, tile_spec, diag_spec, xj_spec, xi_spec]
sweep_call = call(
    sweep_kernel,
    sweep_ins,
    [tile_spec, diag_spec, sums_spec],
    [tiles_shape, diag_shape, sums_shape],
)
last_call = call(sweep_kernel, sweep_ins, [tile_spec, diag_spec], [tiles_shape, diag_shape])


def swapped(value):
    return lax.all_to_all(value, PEERS, split_axis=0, concat_axis=0, tiled=True)


def on_device(omega_tiles, omega_diag, samples, pattern):
    col = lax.axis_index(COL).astype(jnp.int32).reshape(1)
    row, member = pattern // ROWS, pattern % ROWS
    place = (row % Z) // ZL * NP + (row // Z * ZL + row % ZL) * ROWS + member
    place = place.astype(jnp.float32).reshape(1, 1, TILES)
    place = jnp.broadcast_to(
        jnp.pad(place, ((0, 0), (0, 0), (0, BS - TILES))), (NP, 1, BS)
    )
    pieces = jnp.swapaxes(samples.reshape(Q, NP, BS), 0, 1)
    came = swapped(jnp.concatenate([pieces, place, jnp.zeros_like(place)], axis=1))
    listed = came[:, Q, :TILES].astype(jnp.int32)
    own = (
        lax.axis_index("zh") * NP
        + (jnp.arange(NP) // ROWS * ROWS)[:, None]
        + jnp.arange(ROWS)[None, :]
    ).astype(jnp.int32)
    idx = jnp.concatenate([listed, own], axis=1).reshape(NP * WANT)

    def exchanged(mine):
        table = lax.all_gather(mine, "zh").reshape(TABLE, Q, BS)
        got = swapped(select(idx, table).reshape(NP, WANT * Q, BS))
        return got.reshape(NP * WANT * Q, BS)

    def summed(sums):
        got = swapped(sums.reshape(NP, ROWS * Q, BS))
        got = got.reshape(GROUPS, ROWS, ROWS * Q, BS).sum(axis=1)
        return got.reshape(NP, Q, BS)

    xj, xi, sums = first_call(col, exchanged(came[:, :Q]), omega_tiles, omega_diag)
    tiles, diag = omega_tiles, omega_diag
    for sweep in range(ITERS):
        got = exchanged(summed(sums))
        if sweep < ITERS - 1:
            tiles, diag, sums = sweep_call(col, got, tiles, diag, xj, xi)
        else:
            tiles, diag = last_call(col, got, tiles, diag, xj, xi)
    return tiles, diag


def solution(mesh):
    fine = Mesh(mesh.devices.reshape(X, ZH, ZL, Y, CORE), ("x", "zh", "zl", "y", "k"))
    rows = ("x", "zh", "zl")
    in_specs = (
        P(rows, COL, None, None),
        P(rows + COL, None),
        P(rows + COL, None),
        P(rows, COL),
    )
    out_specs = (P(rows, COL, None, None), P(rows + COL, None))
    return jax.shard_map(
        on_device, mesh=fine, in_specs=in_specs, out_specs=out_specs, check_vma=False
    )
```

```python
import jax
import jax.numpy as jnp
from jax import lax
from jax.experimental import pallas as pl
from jax.experimental.pallas import tpu as pltpu
from jax.sharding import Mesh
from jax.sharding import PartitionSpec as P

ITERS = 2
STEP = 0.2
SHRINK = 0.05
RIDGE = 0.1

BS = 128
ROWS = 8
SLOTS = 3
TILES = ROWS * SLOTS
WANT = TILES + ROWS

X, Z, Y, CORE = 4, 16, 4, 2
ZL = 2
ZH = Z // ZL
COL = ("y", "k")
PEERS = ("x", "zl", "y", "k")
NP = X * ZL * Y * CORE
Q = BS // NP
GROUPS = NP // ROWS
TABLE = ZH * NP
PITCH = NP + 8
SENT = 4

VMEM = 48 * 1024 * 1024


def split(v):
    hi = v.astype(jnp.bfloat16)
    lo = (v - hi.astype(jnp.float32)).astype(jnp.bfloat16)
    return hi, lo


def dot(a, b, rhs_dim):
    return lax.dot_general(
        a, b, (((1,), (rhs_dim,)), ((), ())), preferred_element_type=jnp.float32
    )


def shrink(v):
    t = STEP * SHRINK
    return v - jnp.clip(v, -t, t)


def send_kernel(pattern, samples, out):
    for q in range(Q):
        out[pl.ds(q, NP, stride=SENT), :] = samples[q * NP : (q + 1) * NP]
    lane = lax.broadcasted_iota(jnp.int32, (1, BS), 1)
    listed = jnp.zeros((1, BS), jnp.int32)
    for i in range(ROWS):
        for s in range(SLOTS):
            listed = jnp.where(lane == i * SLOTS + s, pattern[s, i], listed)
    listed = jnp.broadcast_to(listed.astype(jnp.float32), (NP, BS))
    for q in range(Q, SENT):
        out[pl.ds(q, NP, stride=SENT), :] = listed


def select_kernel(place, plane, table, out):
    def one(d, carry):
        for t in range(TILES):
            out[d, t] = table[place[d * TILES + t]]
        out[d, TILES:] = table[pl.ds(plane[0] * NP + d // ROWS * ROWS, ROWS)]
        return carry

    lax.fori_loop(0, NP, one, 0, unroll=2)


def reorder(recv, blocks):
    def one(p, carry):
        for w in range(0, WANT * Q, 8):
            part = recv[pl.ds(pl.multiple_of(p * WANT * Q, 8) + w, 8), :]
            blocks[pl.ds(w * PITCH + p, 8, stride=PITCH), :] = part
        return carry

    lax.fori_loop(0, NP, one, 0, unroll=4)


def assembled(blocks, t):
    parts = []
    for q in range(Q):
        start = pl.multiple_of((t * Q + q) * PITCH, 8)
        parts.append(blocks[pl.ds(start, NP), :])
    return jnp.concatenate(parts, axis=0)


def spread(out, i, value):
    for q in range(Q):
        out[pl.ds(i * Q + q, NP, stride=ROWS * Q), :] = value[q * NP : (q + 1) * NP]


def lhs3(pairs):
    return jnp.concatenate([p[n] for n in (0, 0, 1) for p in pairs], axis=1)


def rhs3(pairs, axis):
    return jnp.concatenate([p[n] for n in (0, 1, 0) for p in pairs], axis=axis)


def spread_more(out, i, value):
    for q in range(Q):
        rows = pl.ds(i * Q + q, NP, stride=ROWS * Q)
        out[rows, :] = out[rows, :] + value[q * NP : (q + 1) * NP]


def first_kernel(col, recv, tiles, diag, xj, xi, sums, blocks):
    reorder(recv, blocks)

    def one(i, carry):
        xs = []
        for s in range(SLOTS):
            x = split(assembled(blocks, i * SLOTS + s))
            xs.append(x)
            xj[0, i * SLOTS + s], xj[1, i * SLOTS + s] = x
        xi[0, i], xi[1, i] = split(assembled(blocks, TILES + i))
        bs = [split(tiles[i, s]) for s in range(SLOTS)]
        spread(sums, i, dot(lhs3(bs), rhs3(xs, 0), 0))
        return carry

    lax.fori_loop(0, ROWS, one, 0, unroll=2)
    c = col[0]
    own = (xi[0, c], xi[1, c])
    spread_more(sums, c, dot(lhs3([split(diag[...])]), rhs3([own], 0), 0))


def sweep_kernel(col, recv, tiles, diag, xj, xi, new_tiles, new_diag, *rest):
    *rest, blocks = rest
    reorder(recv, blocks)

    def one(i, carry):
        own_x = (xi[0, i], xi[1, i])
        own_y = split(assembled(blocks, TILES + i))
        lhs = lhs3([own_y, own_x])
        xs = [(xj[0, i * SLOTS + s], xj[1, i * SLOTS + s]) for s in range(SLOTS)]
        ys = [split(assembled(blocks, i * SLOTS + s)) for s in range(SLOTS)]
        rhs = [rhs3([x, y], 1) for x, y in zip(xs, ys)]
        cross = dot(lhs, jnp.concatenate(rhs, axis=0), 1)
        bs = []
        for s in range(SLOTS):
            old = tiles[i, s]
            part = cross[:, s * BS : (s + 1) * BS]
            new = shrink(old - STEP * (part * (0.5 / BS) + RIDGE * old))
            new_tiles[i, s] = new
            bs.append(split(new) if rest else None)
        if rest:
            spread(rest[0], i, dot(lhs3(bs), rhs3(xs, 0), 0))
        return carry

    lax.fori_loop(0, ROWS, one, 0, unroll=ROWS if rest else 2)
    c = col[0]
    own_x = (xi[0, c], xi[1, c])
    own_y = split(assembled(blocks, TILES + c))
    cross = dot(lhs3([own_y, own_x]), rhs3([own_x, own_y], 1), 1)
    old = diag[...]
    shape = (BS, BS)
    eye = lax.broadcasted_iota(jnp.int32, shape, 0) == lax.broadcasted_iota(
        jnp.int32, shape, 1
    )
    pivots = jnp.where(eye, 1.0 / jnp.where(eye, old, 1.0), 0.0)
    stepped = old - STEP * (cross * (0.5 / BS) + RIDGE * old - pivots)
    new = jnp.where(eye, stepped, shrink(stepped))
    new_diag[...] = new
    if rest:
        spread_more(rest[0], c, dot(lhs3([split(new)]), rhs3([own_x], 0), 0))


in_smem = pl.BlockSpec(memory_space=pltpu.SMEM)
in_vmem = pl.BlockSpec(memory_space=pltpu.VMEM)
FLOAT, HALF = jnp.float32, jnp.bfloat16
TABLE_SHAPE = (TABLE, Q, BS)
BLOCKS = pltpu.VMEM((WANT * Q * PITCH, BS), FLOAT)


def call(kernel, scalars, arrays, outputs, scratch=()):
    shapes = [jax.ShapeDtypeStruct(o, t) for o, t in outputs]
    several = len(shapes) > 1
    return pl.pallas_call(
        kernel,
        in_specs=[in_smem] * scalars + [in_vmem] * arrays,
        out_specs=[in_vmem] * len(shapes) if several else in_vmem,
        out_shape=shapes if several else shapes[0],
        scratch_shapes=scratch,
        compiler_params=pltpu.CompilerParams(vmem_limit_bytes=VMEM),
    )


send = call(send_kernel, 1, 1, [((NP * SENT, BS), FLOAT)])
select = call(select_kernel, 2, 1, [((NP, WANT, Q, BS), FLOAT)])
xs_out = [((2, TILES, BS, BS), HALF), ((2, ROWS, BS, BS), HALF)]
new_out = [((ROWS, SLOTS, BS, BS), FLOAT), ((BS, BS), FLOAT)]
sums_out = [((NP * ROWS * Q, BS), FLOAT)]
first_call = call(first_kernel, 1, 3, xs_out + sums_out, [BLOCKS])
sweep_call = call(sweep_kernel, 1, 5, new_out + sums_out, [BLOCKS])
last_call = call(sweep_kernel, 1, 5, new_out, [BLOCKS])


def swapped(value, rows):
    return lax.all_to_all(
        value.reshape(NP, rows, BS), PEERS, split_axis=0, concat_axis=0, tiled=True
    )


def on_device(omega_tiles, omega_diag, samples, pattern):
    col = lax.axis_index(COL).astype(jnp.int32).reshape(1)
    plane = lax.axis_index("zh").astype(jnp.int32).reshape(1)
    came = swapped(send(pattern.T, samples), SENT)
    block = came[:, Q, :TILES].astype(jnp.int32)
    row, member = block // ROWS, block % ROWS
    place = (row % Z) // ZL * NP + (row // Z * ZL + row % ZL) * ROWS + member
    place = place.reshape(NP * TILES)

    def exchanged(mine):
        table = lax.all_gather(mine, "zh").reshape(TABLE_SHAPE)
        got = swapped(select(place, plane, table), WANT * Q)
        return got.reshape(NP * WANT * Q, BS)

    got = exchanged(came[:, :Q].reshape(NP * Q, BS))
    xj, xi, sums = first_call(col, got, omega_tiles, omega_diag)
    tiles, diag = omega_tiles, omega_diag
    for sweep in range(ITERS):
        parts = swapped(sums, ROWS * Q).reshape(GROUPS, ROWS, ROWS * Q, BS)
        got = exchanged(parts.sum(axis=1).reshape(NP * Q, BS))
        if sweep < ITERS - 1:
            tiles, diag, sums = sweep_call(col, got, tiles, diag, xj, xi)
        else:
            tiles, diag = last_call(col, got, tiles, diag, xj, xi)
    return tiles, diag


def solution(mesh):
    fine = Mesh(mesh.devices.reshape(X, ZH, ZL, Y, CORE), ("x", "zh", "zl", "y", "k"))
    rows = ("x", "zh", "zl")
    in_specs = (
        P(rows, COL, None, None),
        P(rows + COL, None),
        P(rows + COL, None),
        P(rows, COL),
    )
    out_specs = (P(rows, COL, None, None), P(rows + COL, None))
    return jax.shard_map(
        on_device, mesh=fine, in_specs=in_specs, out_specs=out_specs, check_vma=False
    )
```

```python
import functools

import jax
import jax.numpy as jnp
from jax import lax
from jax.experimental import pallas as pl
from jax.experimental.pallas import tpu as pltpu
from jax.sharding import Mesh
from jax.sharding import PartitionSpec as P

ITERS = 2
STEP = 0.2
SHRINK = 0.05
RIDGE = 0.1

BS = 128
ROWS = 8
SLOTS = 3
TILES = ROWS * SLOTS
OWN = ROWS // 2
WIDE = 2 * SLOTS
WANT = TILES + OWN

X, Z, Y, CORE = 4, 16, 4, 2
ZL = 2
ZH = Z // ZL
COL = ("y", "k")
PEERS = ("x", "zl", "k", "y")
NP = X * ZL * Y * CORE
Q = BS // NP
GROUPS = NP // ROWS
TABLE = ZH * NP
PITCH = NP + 8
SENT = 4

VMEM = 48 * 1024 * 1024


def split(v):
    hi = v.astype(jnp.bfloat16)
    lo = (v - hi.astype(jnp.float32)).astype(jnp.bfloat16)
    return hi, lo


def dot(a, b, rhs_dim):
    return lax.dot_general(
        a, b, (((1,), (rhs_dim,)), ((), ())), preferred_element_type=jnp.float32
    )


def turned(member):
    return member % CORE * Y + member // CORE


def shrink(v):
    t = STEP * SHRINK
    return v - jnp.clip(v, -t, t)


def send_kernel(pattern, samples, out, numbers, block, sems):
    copies = loading([samples, pattern], [block, numbers], sems)
    copies[0].wait()
    for q in range(Q):
        out[pl.ds(q, NP, stride=SENT), :] = block[q * NP : (q + 1) * NP]
    copies[1].wait()
    lane = lax.broadcasted_iota(jnp.int32, (1, BS), 1)
    listed = jnp.zeros((1, BS), jnp.int32)
    for i in range(ROWS):
        for s in range(SLOTS):
            listed = jnp.where(lane == i * SLOTS + s, numbers[s, i], listed)
    listed = jnp.broadcast_to(listed.astype(jnp.float32), (NP, BS))
    for q in range(Q, SENT):
        out[pl.ds(q, NP, stride=SENT), :] = listed


def select_kernel(place, plane, table, out, numbers, sems):
    [copy] = loading([place], [numbers], sems)

    def rows(d, carry):
        out[d, TILES:] = table[pl.ds(plane[0] * NP + d // OWN * OWN, OWN)]
        return carry

    lax.fori_loop(0, NP, rows, 0, unroll=4)
    copy.wait()

    def columns(n, carry):
        pair = n // Y * ROWS + n % Y
        pair = (pair, pair + Y)
        bases = [peer * TILES for peer in pair]
        for core in range(CORE):
            for t in range(TILES):
                base = bases[core ^ t % WIDE // SLOTS]
                entry = t // WIDE * CORE * SLOTS + core * SLOTS + t % SLOTS
                out[pair[core], t] = table[numbers[base + entry]]
        return carry

    lax.fori_loop(0, NP // CORE, columns, 0)


def loading(sources, places, sems):
    copies = []
    for n, (source, place) in enumerate(zip(sources, places)):
        copies.append(pltpu.make_async_copy(source, place, sems.at[n]))
        copies[n].start()
    return copies


def reorder(recv, blocks):
    def one(p, carry):
        for w in range(0, WANT * Q, 8):
            part = recv[pl.ds(pl.multiple_of(p * WANT * Q, 8) + w, 8), :]
            blocks[pl.ds(w * PITCH + p, 8, stride=PITCH), :] = part
        return carry

    lax.fori_loop(0, NP, one, 0, unroll=4)


def assembled(blocks, t):
    parts = []
    for q in range(Q):
        start = pl.multiple_of((t * Q + q) * PITCH, 8)
        parts.append(blocks[pl.ds(start, NP), :])
    return jnp.concatenate(parts, axis=0)


def spread(out, i, value, add=False):
    each = out.shape[0] // NP
    for q in range(Q):
        rows = pl.ds(i * Q + q, NP, stride=each)
        part = value[q * NP : (q + 1) * NP]
        out[rows, :] = out[rows, :] + part if add else part


def lhs3(pairs):
    return jnp.concatenate([p[n] for n in (0, 0, 1) for p in pairs], axis=1)


def rhs3(pairs, axis):
    return jnp.concatenate([p[n] for n in (0, 1, 0) for p in pairs], axis=axis)


def first_kernel(at, recv, tiles, other, diag, xj, xi, held, sums, blocks):
    reorder(recv, blocks)

    def one(i, carry):
        xs, bs = [], []
        for s in range(WIDE):
            x = split(assembled(blocks, i * WIDE + s))
            xs.append(x)
            xj[0, i * WIDE + s], xj[1, i * WIDE + s] = x
            b = tiles[i * CORE + at[0], s] if s < SLOTS else other[i, s - SLOTS]
            held[i, s] = b
            bs.append(split(b))
        xi[0, i], xi[1, i] = split(assembled(blocks, TILES + i))
        spread(sums, i, dot(lhs3(bs), rhs3(xs, 0), 0))
        return carry

    lax.fori_loop(0, OWN, one, 0, unroll=FIRST_UNROLL)
    c = at[1]
    own = (xi[0, c], xi[1, c])
    spread(sums, c, dot(lhs3([split(diag[...])]), rhs3([own], 0), 0), add=True)


def sweep_kernel(last, at, recv, tiles, diag, xj, xi, *rest):
    *new_tiles, new_diag, sums, blocks = rest if not last else (*rest[:-1], None, rest[-1])
    reorder(recv, blocks)

    def one(i, carry):
        own_x = (xi[0, i], xi[1, i])
        own_y = split(assembled(blocks, TILES + i))
        lhs = lhs3([own_y, own_x])
        bs, xs = [], []
        for half in range(2):
            at_half = range(half * SLOTS, (half + 1) * SLOTS)
            half_xs = [(xj[0, i * WIDE + s], xj[1, i * WIDE + s]) for s in at_half]
            ys = [split(assembled(blocks, i * WIDE + s)) for s in at_half]
            rhs = [rhs3([x, y], 1) for x, y in zip(half_xs, ys)]
            cross = dot(lhs, jnp.concatenate(rhs, axis=0), 1)
            xs += half_xs
            for n, s in enumerate(at_half):
                old = tiles[i, s]
                part = cross[:, n * BS : (n + 1) * BS]
                new = shrink(old - STEP * (part * (0.5 / BS) + RIDGE * old))
                if last:
                    new_tiles[half][i, n] = new
                else:
                    new_tiles[0][i, s] = new
                    bs.append(split(new))
        if not last:
            spread(sums, i, dot(lhs3(bs), rhs3(xs, 0), 0))
        return carry

    lax.fori_loop(0, OWN, one, 0, unroll=OWN)
    c = at[1]
    own_x = (xi[0, c], xi[1, c])
    own_y = split(assembled(blocks, TILES + c))
    cross = dot(lhs3([own_y, own_x]), rhs3([own_x, own_y], 1), 1)
    old = diag[...]
    shape = (BS, BS)
    eye = lax.broadcasted_iota(jnp.int32, shape, 0) == lax.broadcasted_iota(
        jnp.int32, shape, 1
    )
    pivots = jnp.where(eye, 1.0 / jnp.where(eye, old, 1.0), 0.0)
    stepped = old - STEP * (cross * (0.5 / BS) + RIDGE * old - pivots)
    new = jnp.where(eye, stepped, shrink(stepped))
    new_diag[...] = new
    if not last:
        spread(sums, c, dot(lhs3([split(new)]), rhs3([own_x], 0), 0), add=True)


FIRST_UNROLL = 2
SPACES = {
    "s": pl.BlockSpec(memory_space=pltpu.SMEM),
    "v": pl.BlockSpec(memory_space=pltpu.VMEM),
    "a": pl.BlockSpec(memory_space=pl.ANY),
}
FLOAT, HALF = jnp.float32, jnp.bfloat16
TABLE_SHAPE = (TABLE, Q, BS)
DIAG = (BS, BS)


def sems(count):
    return pltpu.SemaphoreType.DMA((count,))


def floats(*shape):
    return pltpu.VMEM(shape, FLOAT)


def call(kernel, takes, gives, outputs, scratch):
    shapes = [jax.ShapeDtypeStruct(o, t) for o, t in outputs]
    several = len(shapes) > 1
    specs = [SPACES[g] for g in gives]
    return pl.pallas_call(
        kernel,
        in_specs=[SPACES[t] for t in takes],
        out_specs=specs if several else specs[0],
        out_shape=shapes if several else shapes[0],
        scratch_shapes=scratch,
        compiler_params=pltpu.CompilerParams(vmem_limit_bytes=VMEM),
    )


send = call(
    send_kernel,
    "aa",
    "v",
    [((NP * SENT, BS), FLOAT)],
    [pltpu.SMEM((SLOTS, ROWS), jnp.int32), floats(*DIAG), sems(2)],
)
select = call(
    select_kernel,
    "asv",
    "v",
    [((NP, WANT, Q, BS), FLOAT)],
    [pltpu.SMEM((NP * TILES,), jnp.int32), sems(1)],
)
blocks = [floats(WANT * Q * PITCH, BS)]
xs_out = [((2, TILES, BS, BS), HALF), ((2, OWN, BS, BS), HALF)]
held_out = [((OWN, WIDE, BS, BS), FLOAT)]
half_out = [((OWN, SLOTS, BS, BS), FLOAT)] * 2
diag_out = [(DIAG, FLOAT)]
sums_out = [((NP * OWN * Q, BS), FLOAT)]
middle, final = (functools.partial(sweep_kernel, last) for last in (False, True))
first_call = call(first_kernel, "svvvv", "vvvv", xs_out + held_out + sums_out, blocks)
sweep_call = call(middle, "svvvvv", "vvv", held_out + diag_out + sums_out, blocks)
last_call = call(final, "svvvvv", "vvv", half_out + diag_out, blocks)


def to_mate(value):
    return lax.ppermute(value, "k", [(0, 1), (1, 0)])


def swapped(value):
    flat = value.reshape(NP, -1, BS)
    return lax.all_to_all(flat, PEERS, split_axis=0, concat_axis=0, tiled=True)


def on_device(omega_tiles, omega_diag, samples, pattern):
    core = lax.axis_index("k").astype(jnp.int32)
    at = jnp.stack([core, lax.axis_index("y").astype(jnp.int32)])
    in_pairs = omega_tiles.reshape(OWN, CORE, SLOTS, BS, BS)
    other = to_mate(jnp.where(core == 0, in_pairs[:, 1], in_pairs[:, 0]))
    plane = lax.axis_index("zh").astype(jnp.int32).reshape(1)
    came = swapped(send(pattern.T, samples))
    block = came[:, Q, :TILES].astype(jnp.int32)
    row, member = block // ROWS, block % ROWS
    place = (row % Z) // ZL * NP + (row // Z * ZL + row % ZL) * ROWS + turned(member)
    place = place.reshape(NP * TILES)

    def exchanged(mine):
        table = lax.all_gather(mine.reshape(NP * Q, BS), "zh").reshape(TABLE_SHAPE)
        return swapped(select(place, plane, table)).reshape(NP * WANT * Q, BS)

    got = exchanged(came[:, :Q])
    xj, xi, tiles, sums = first_call(at, got, omega_tiles, other, omega_diag)
    diag = omega_diag
    for sweep in range(ITERS):
        parts = swapped(sums).reshape(GROUPS, CORE, Y, OWN * Q, BS)
        got = exchanged(parts.sum(axis=2))
        if sweep < ITERS - 1:
            tiles, diag, sums = sweep_call(at, got, tiles, diag, xj, xi)
        else:
            kept, given, diag = last_call(at, got, tiles, diag, xj, xi)
    taken = to_mate(given)
    even = jnp.where(core == 0, kept, taken)
    odd = jnp.where(core == 0, taken, kept)
    return jnp.stack([even, odd], axis=1).reshape(omega_tiles.shape), diag


def solution(mesh):
    fine = Mesh(mesh.devices.reshape(X, ZH, ZL, Y, CORE), ("x", "zh", "zl", "y", "k"))
    rows = ("x", "zh", "zl")
    in_specs = (
        P(rows, COL, None, None),
        P(rows + COL, None),
        P(rows + COL, None),
        P(rows, COL),
    )
    out_specs = (P(rows, COL, None, None), P(rows + COL, None))
    return jax.shard_map(
        on_device, mesh=fine, in_specs=in_specs, out_specs=out_specs, check_vma=False
    )
```

```python
import functools

import jax
import jax.numpy as jnp
from jax import lax
from jax.experimental import pallas as pl
from jax.experimental.pallas import tpu as pltpu
from jax.sharding import Mesh
from jax.sharding import PartitionSpec as P

ITERS = 2
STEP = 0.2
SHRINK = 0.05
RIDGE = 0.1

BS = 128
ROWS = 8
SLOTS = 3
TILES = ROWS * SLOTS
OWN = ROWS // 2
WIDE = 2 * SLOTS
WANT = TILES + OWN

X, Z, Y, CORE = 4, 16, 4, 2
ZL = 2
ZH = Z // ZL
COL = ("y", "k")
PEERS = ("x", "zl", "k", "y")
NP = X * ZL * Y * CORE
Q = BS // NP
GROUPS = NP // ROWS
TABLE = ZH * NP
PITCH = NP + 8
SENT = 4

VMEM = 48 * 1024 * 1024


def split(v):
    hi = v.astype(jnp.bfloat16)
    lo = (v - hi.astype(jnp.float32)).astype(jnp.bfloat16)
    return hi, lo


def dot(a, b, rhs_dim):
    return lax.dot_general(
        a, b, (((1,), (rhs_dim,)), ((), ())), preferred_element_type=jnp.float32
    )


def turned(member):
    return member % CORE * Y + member // CORE


def shrink(v):
    t = STEP * SHRINK
    return v - jnp.clip(v, -t, t)


def send_kernel(pattern, samples, out, numbers, block, sems):
    copies = loading([samples, pattern], [block, numbers], sems)
    copies[0].wait()
    for q in range(Q):
        out[pl.ds(q, NP, stride=SENT), :] = block[q * NP : (q + 1) * NP]
    copies[1].wait()
    lane = lax.broadcasted_iota(jnp.int32, (1, BS), 1)
    listed = jnp.zeros((1, BS), jnp.int32)
    for i in range(ROWS):
        for s in range(SLOTS):
            listed = jnp.where(lane == i * SLOTS + s, numbers[s, i], listed)
    listed = jnp.broadcast_to(listed.astype(jnp.float32), (NP, BS))
    for q in range(Q, SENT):
        out[pl.ds(q, NP, stride=SENT), :] = listed


def select_kernel(place, plane, table, out, numbers, sems):
    [copy] = loading([place], [numbers], sems)

    def rows(d, carry):
        out[d, TILES:] = table[pl.ds(plane[0] * NP + d // OWN * OWN, OWN)]
        return carry

    lax.fori_loop(0, NP, rows, 0, unroll=4)
    copy.wait()

    def columns(n, carry):
        pair = n // Y * ROWS + n % Y
        pair = (pair, pair + Y)
        bases = [peer * TILES for peer in pair]
        for core in range(CORE):
            for t in range(TILES):
                base = bases[core ^ t % WIDE // SLOTS]
                entry = t // WIDE * CORE * SLOTS + core * SLOTS + t % SLOTS
                out[pair[core], t] = table[numbers[base + entry]]
        return carry

    lax.fori_loop(0, NP // CORE, columns, 0)


def loading(sources, places, sems):
    copies = []
    for n, (source, place) in enumerate(zip(sources, places)):
        copies.append(pltpu.make_async_copy(source, place, sems.at[n]))
        copies[n].start()
    return copies


def reorder(recv, blocks):
    def one(p, carry):
        for w in range(0, WANT * Q, 8):
            part = recv[pl.ds(pl.multiple_of(p * WANT * Q, 8) + w, 8), :]
            blocks[pl.ds(w * PITCH + p, 8, stride=PITCH), :] = part
        return carry

    lax.fori_loop(0, NP, one, 0, unroll=4)


def assembled(blocks, t):
    parts = []
    for q in range(Q):
        start = pl.multiple_of((t * Q + q) * PITCH, 8)
        parts.append(blocks[pl.ds(start, NP), :])
    return jnp.concatenate(parts, axis=0)


def spread(out, i, value, add=False):
    each = out.shape[0] // NP
    for q in range(Q):
        rows = pl.ds(i * Q + q, NP, stride=each)
        part = value[q * NP : (q + 1) * NP]
        out[rows, :] = out[rows, :] + part if add else part


def lhs3(pairs):
    return jnp.concatenate([p[n] for n in (0, 0, 1) for p in pairs], axis=1)


def rhs3(pairs, axis):
    return jnp.concatenate([p[n] for n in (0, 1, 0) for p in pairs], axis=axis)


def first_kernel(at, recv, tiles, other, diag, xj, xi, held, sums, blocks):
    reorder(recv, blocks)

    def one(i, carry):
        xs, bs = [], []
        for s in range(WIDE):
            x = split(assembled(blocks, i * WIDE + s))
            xs.append(x)
            xj[0, i * WIDE + s], xj[1, i * WIDE + s] = x
            b = tiles[i * CORE + at[0], s] if s < SLOTS else other[i, s - SLOTS]
            held[i, s] = b
            bs.append(split(b))
        xi[0, i], xi[1, i] = split(assembled(blocks, TILES + i))
        spread(sums, i, dot(lhs3(bs), rhs3(xs, 0), 0))
        return carry

    lax.fori_loop(0, OWN, one, 0, unroll=FIRST_UNROLL)
    c = at[1]
    own = (xi[0, c], xi[1, c])
    spread(sums, c, dot(lhs3([split(diag[...])]), rhs3([own], 0), 0), add=True)


def sweep_kernel(last, at, recv, tiles, diag, xj, xi, *rest):
    *new_tiles, new_diag, sums, blocks = rest if not last else (*rest[:-1], None, rest[-1])
    reorder(recv, blocks)

    def one(i, carry):
        own_x = (xi[0, i], xi[1, i])
        own_y = split(assembled(blocks, TILES + i))
        lhs = lhs3([own_y, own_x])
        bs, xs = [], []
        for half in range(2):
            at_half = range(half * SLOTS, (half + 1) * SLOTS)
            half_xs = [(xj[0, i * WIDE + s], xj[1, i * WIDE + s]) for s in at_half]
            ys = [split(assembled(blocks, i * WIDE + s)) for s in at_half]
            rhs = [rhs3([x, y], 1) for x, y in zip(half_xs, ys)]
            cross = dot(lhs, jnp.concatenate(rhs, axis=0), 1)
            xs += half_xs
            for n, s in enumerate(at_half):
                old = tiles[i, s]
                part = cross[:, n * BS : (n + 1) * BS]
                new = shrink(old - STEP * (part * (0.5 / BS) + RIDGE * old))
                if last:
                    new_tiles[half][i, n] = new
                else:
                    new_tiles[0][i, s] = new
                    bs.append(split(new))
        if not last:
            spread(sums, i, dot(lhs3(bs), rhs3(xs, 0), 0))
        return carry

    lax.fori_loop(0, OWN, one, 0, unroll=OWN)
    c = at[1]
    own_x = (xi[0, c], xi[1, c])
    own_y = split(assembled(blocks, TILES + c))
    cross = dot(lhs3([own_y, own_x]), rhs3([own_x, own_y], 1), 1)
    old = diag[...]
    shape = (BS, BS)
    eye = lax.broadcasted_iota(jnp.int32, shape, 0) == lax.broadcasted_iota(
        jnp.int32, shape, 1
    )
    pivots = jnp.where(eye, 1.0 / jnp.where(eye, old, 1.0), 0.0)
    stepped = old - STEP * (cross * (0.5 / BS) + RIDGE * old - pivots)
    new = jnp.where(eye, stepped, shrink(stepped))
    new_diag[...] = new
    if not last:
        spread(sums, c, dot(lhs3([split(new)]), rhs3([own_x], 0), 0), add=True)


FIRST_UNROLL = 2
def merge_kernel(at, kept, taken, out, sems):
    mine, other = out.at[:, at[0]], out.at[:, 1 - at[0]]
    for copy in loading([kept, taken], [mine, other], sems):
        copy.wait()


SPACES = {
    "s": pl.BlockSpec(memory_space=pltpu.SMEM),
    "v": pl.BlockSpec(memory_space=pltpu.VMEM),
    "a": pl.BlockSpec(memory_space=pl.ANY),
}
FLOAT, HALF = jnp.float32, jnp.bfloat16
TABLE_SHAPE = (TABLE, Q, BS)
DIAG = (BS, BS)


def sems(count):
    return pltpu.SemaphoreType.DMA((count,))


def floats(*shape):
    return pltpu.VMEM(shape, FLOAT)


def call(kernel, takes, gives, outputs, scratch):
    shapes = [jax.ShapeDtypeStruct(o, t) for o, t in outputs]
    several = len(shapes) > 1
    specs = [SPACES[g] for g in gives]
    return pl.pallas_call(
        kernel,
        in_specs=[SPACES[t] for t in takes],
        out_specs=specs if several else specs[0],
        out_shape=shapes if several else shapes[0],
        scratch_shapes=scratch,
        compiler_params=pltpu.CompilerParams(vmem_limit_bytes=VMEM),
    )


send = call(
    send_kernel,
    "aa",
    "v",
    [((NP * SENT, BS), FLOAT)],
    [pltpu.SMEM((SLOTS, ROWS), jnp.int32), floats(*DIAG), sems(2)],
)
select = call(
    select_kernel,
    "asv",
    "v",
    [((NP, WANT, Q, BS), FLOAT)],
    [pltpu.SMEM((NP * TILES,), jnp.int32), sems(1)],
)
blocks = [floats(WANT * Q * PITCH, BS)]
xs_out = [((2, TILES, BS, BS), HALF), ((2, OWN, BS, BS), HALF)]
held_out = [((OWN, WIDE, BS, BS), FLOAT)]
half_out = [((OWN, SLOTS, BS, BS), FLOAT)] * 2
diag_out = [(DIAG, FLOAT)]
sums_out = [((NP * OWN * Q, BS), FLOAT)]
middle, final = (functools.partial(sweep_kernel, last) for last in (False, True))
first_call = call(first_kernel, "svvvv", "vvvv", xs_out + held_out + sums_out, blocks)
sweep_call = call(middle, "svvvvv", "vvv", held_out + diag_out + sums_out, blocks)
last_call = call(final, "svvvvv", "vvv", half_out + diag_out, blocks)


merge = call(merge_kernel, "saa", "a", [((OWN, CORE, SLOTS, BS, BS), FLOAT)], [sems(2)])


def to_mate(value):
    return lax.ppermute(value, "k", [(0, 1), (1, 0)])


def swapped(value):
    flat = value.reshape(NP, -1, BS)
    return lax.all_to_all(flat, PEERS, split_axis=0, concat_axis=0, tiled=True)


def on_device(omega_tiles, omega_diag, samples, pattern):
    core = lax.axis_index("k").astype(jnp.int32)
    at = jnp.stack([core, lax.axis_index("y").astype(jnp.int32)])
    in_pairs = omega_tiles.reshape(OWN, CORE, SLOTS, BS, BS)
    other = to_mate(jnp.where(core == 0, in_pairs[:, 1], in_pairs[:, 0]))
    plane = lax.axis_index("zh").astype(jnp.int32).reshape(1)
    came = swapped(send(pattern.T, samples))
    block = came[:, Q, :TILES].astype(jnp.int32)
    row, member = block // ROWS, block % ROWS
    place = (row % Z) // ZL * NP + (row // Z * ZL + row % ZL) * ROWS + turned(member)
    place = place.reshape(NP * TILES)

    def exchanged(mine):
        table = lax.all_gather(mine.reshape(NP * Q, BS), "zh").reshape(TABLE_SHAPE)
        return swapped(select(place, plane, table)).reshape(NP * WANT * Q, BS)

    got = exchanged(came[:, :Q])
    xj, xi, tiles, sums = first_call(at, got, omega_tiles, other, omega_diag)
    diag = omega_diag
    for sweep in range(ITERS):
        parts = swapped(sums).reshape(GROUPS, CORE, Y, OWN * Q, BS)
        got = exchanged(parts.sum(axis=2))
        if sweep < ITERS - 1:
            tiles, diag, sums = sweep_call(at, got, tiles, diag, xj, xi)
        else:
            kept, given, diag = last_call(at, got, tiles, diag, xj, xi)
    taken = to_mate(given)
    return merge(at, kept, taken).reshape(omega_tiles.shape), diag


def solution(mesh):
    fine = Mesh(mesh.devices.reshape(X, ZH, ZL, Y, CORE), ("x", "zh", "zl", "y", "k"))
    rows = ("x", "zh", "zl")
    in_specs = (
        P(rows, COL, None, None),
        P(rows + COL, None),
        P(rows + COL, None),
        P(rows, COL),
    )
    out_specs = (P(rows, COL, None, None), P(rows + COL, None))
    return jax.shard_map(
        on_device, mesh=fine, in_specs=in_specs, out_specs=out_specs, check_vma=False
    )
```

```python
import functools

import jax
import jax.numpy as jnp
from jax import lax
from jax.experimental import pallas as pl
from jax.experimental.pallas import tpu as pltpu
from jax.sharding import Mesh
from jax.sharding import PartitionSpec as P

ITERS = 2
STEP = 0.2
SHRINK = 0.05
RIDGE = 0.1

BS = 128
ROWS = 8
SLOTS = 3
TILES = ROWS * SLOTS
OWN = ROWS // 2
WIDE = 2 * SLOTS
WANT = TILES + OWN

X, Z, Y, CORE = 4, 16, 4, 2
ZL = 2
ZH = Z // ZL
COL = ("y", "k")
PEERS = ("x", "zl", "k", "y")
NP = X * ZL * Y * CORE
Q = BS // NP
GROUPS = NP // ROWS
TABLE = ZH * NP
PITCH = NP + 8
SENT = 4

VMEM = 48 * 1024 * 1024


def split(v):
    hi = v.astype(jnp.bfloat16)
    lo = (v - hi.astype(jnp.float32)).astype(jnp.bfloat16)
    return hi, lo


def dot(a, b, rhs_dim):
    return lax.dot_general(
        a, b, (((1,), (rhs_dim,)), ((), ())), preferred_element_type=jnp.float32
    )


def turned(member):
    return member % CORE * Y + member // CORE


def shrink(v):
    t = STEP * SHRINK
    return v - jnp.clip(v, -t, t)


def send_kernel(pattern, samples, out, numbers, block, sems):
    copies = loading([samples, pattern], [block, numbers], sems)
    copies[0].wait()
    for q in range(Q):
        out[pl.ds(q, NP, stride=SENT), :] = block[q * NP : (q + 1) * NP]
    copies[1].wait()
    lane = lax.broadcasted_iota(jnp.int32, (1, BS), 1)
    listed = jnp.zeros((1, BS), jnp.int32)
    for i in range(ROWS):
        for s in range(SLOTS):
            listed = jnp.where(lane == i * SLOTS + s, numbers[s, i], listed)
    listed = jnp.broadcast_to(listed.astype(jnp.float32), (NP, BS))
    for q in range(Q, SENT):
        out[pl.ds(q, NP, stride=SENT), :] = listed


def select_kernel(chunks, place, plane, table, target, *rest):
    *out, numbers, sems = rest
    out = out[0] if chunks else target
    [copy] = loading([place], [numbers], sems)

    def rows(d, carry):
        out[d, TILES:] = table[pl.ds(plane[0] * NP + d // OWN * OWN, OWN)]
        return carry

    lax.fori_loop(0, NP, rows, 0, unroll=4)
    copy.wait()

    def columns(n, carry):
        pair = n // Y * ROWS + n % Y
        pair = (pair, pair + Y)
        bases = [peer * TILES for peer in pair]
        for core in range(CORE):
            for t in range(TILES):
                base = bases[core ^ t % WIDE // SLOTS]
                entry = t // WIDE * CORE * SLOTS + core * SLOTS + t % SLOTS
                out[pair[core], t] = table[numbers[base + entry]]
        return carry

    if not chunks:
        lax.fori_loop(0, NP // CORE, columns, 0)
        return
    stores = []
    for n in range(chunks):
        count = NP // CORE // chunks
        lax.fori_loop(n * count, (n + 1) * count, columns, 0)
        peers = pl.ds(n * count * CORE, count * CORE)
        stores.append(pltpu.make_async_copy(out.at[peers], target.at[peers], sems.at[1 + n]))
        stores[n].start()
    for store in stores:
        store.wait()


def loading(sources, places, sems):
    copies = []
    for n, (source, place) in enumerate(zip(sources, places)):
        copies.append(pltpu.make_async_copy(source, place, sems.at[n]))
        copies[n].start()
    return copies


def reorder(recv, blocks):
    def one(p, carry):
        for w in range(0, WANT * Q, 8):
            part = recv[pl.ds(pl.multiple_of(p * WANT * Q, 8) + w, 8), :]
            blocks[pl.ds(w * PITCH + p, 8, stride=PITCH), :] = part
        return carry

    lax.fori_loop(0, NP, one, 0, unroll=4)


def assembled(blocks, t):
    parts = []
    for q in range(Q):
        start = pl.multiple_of((t * Q + q) * PITCH, 8)
        parts.append(blocks[pl.ds(start, NP), :])
    return jnp.concatenate(parts, axis=0)


def spread(out, i, value, add=False):
    each = out.shape[0] // NP
    for q in range(Q):
        rows = pl.ds(i * Q + q, NP, stride=each)
        part = value[q * NP : (q + 1) * NP]
        out[rows, :] = out[rows, :] + part if add else part


def lhs3(pairs):
    return jnp.concatenate([p[n] for n in (0, 0, 1) for p in pairs], axis=1)


def rhs3(pairs, axis):
    return jnp.concatenate([p[n] for n in (0, 1, 0) for p in pairs], axis=axis)


def first_kernel(at, recv, tiles, other, diag, xj, xi, held, sums, blocks):
    reorder(recv, blocks)

    def one(i, carry):
        xs, bs = [], []
        for s in range(WIDE):
            x = split(assembled(blocks, i * WIDE + s))
            xs.append(x)
            xj[0, i * WIDE + s], xj[1, i * WIDE + s] = x
            b = tiles[i * CORE + at[0], s] if s < SLOTS else other[i, s - SLOTS]
            held[i, s] = b
            bs.append(split(b))
        xi[0, i], xi[1, i] = split(assembled(blocks, TILES + i))
        spread(sums, i, dot(lhs3(bs), rhs3(xs, 0), 0))
        return carry

    lax.fori_loop(0, OWN, one, 0, unroll=FIRST_UNROLL)
    c = at[1]
    own = (xi[0, c], xi[1, c])
    spread(sums, c, dot(lhs3([split(diag[...])]), rhs3([own], 0), 0), add=True)


def sweep_kernel(last, at, recv, tiles, diag, xj, xi, *rest):
    *new_tiles, new_diag, sums, blocks = rest if not last else (*rest[:-1], None, rest[-1])
    reorder(recv, blocks)

    def one(i, carry):
        own_x = (xi[0, i], xi[1, i])
        own_y = split(assembled(blocks, TILES + i))
        lhs = lhs3([own_y, own_x])
        bs, xs = [], []
        for half in range(2):
            at_half = range(half * SLOTS, (half + 1) * SLOTS)
            half_xs = [(xj[0, i * WIDE + s], xj[1, i * WIDE + s]) for s in at_half]
            ys = [split(assembled(blocks, i * WIDE + s)) for s in at_half]
            rhs = [rhs3([x, y], 1) for x, y in zip(half_xs, ys)]
            cross = dot(lhs, jnp.concatenate(rhs, axis=0), 1)
            xs += half_xs
            for n, s in enumerate(at_half):
                old = tiles[i, s]
                part = cross[:, n * BS : (n + 1) * BS]
                new = shrink(old - STEP * (part * (0.5 / BS) + RIDGE * old))
                if last:
                    new_tiles[half][i, n] = new
                else:
                    new_tiles[0][i, s] = new
                    bs.append(split(new))
        if not last:
            spread(sums, i, dot(lhs3(bs), rhs3(xs, 0), 0))
        return carry

    lax.fori_loop(0, OWN, one, 0, unroll=OWN)
    c = at[1]
    own_x = (xi[0, c], xi[1, c])
    own_y = split(assembled(blocks, TILES + c))
    cross = dot(lhs3([own_y, own_x]), rhs3([own_x, own_y], 1), 1)
    old = diag[...]
    shape = (BS, BS)
    eye = lax.broadcasted_iota(jnp.int32, shape, 0) == lax.broadcasted_iota(
        jnp.int32, shape, 1
    )
    pivots = jnp.where(eye, 1.0 / jnp.where(eye, old, 1.0), 0.0)
    stepped = old - STEP * (cross * (0.5 / BS) + RIDGE * old - pivots)
    new = jnp.where(eye, stepped, shrink(stepped))
    new_diag[...] = new
    if not last:
        spread(sums, c, dot(lhs3([split(new)]), rhs3([own_x], 0), 0), add=True)


FIRST_UNROLL = 2
SPACES = {
    "s": pl.BlockSpec(memory_space=pltpu.SMEM),
    "v": pl.BlockSpec(memory_space=pltpu.VMEM),
    "a": pl.BlockSpec(memory_space=pl.ANY),
}
FLOAT, HALF = jnp.float32, jnp.bfloat16
TABLE_SHAPE = (TABLE, Q, BS)
DIAG = (BS, BS)


def sems(count):
    return pltpu.SemaphoreType.DMA((count,))


def floats(*shape):
    return pltpu.VMEM(shape, FLOAT)


def call(kernel, takes, gives, outputs, scratch):
    shapes = [jax.ShapeDtypeStruct(o, t) for o, t in outputs]
    several = len(shapes) > 1
    specs = [SPACES[g] for g in gives]
    return pl.pallas_call(
        kernel,
        in_specs=[SPACES[t] for t in takes],
        out_specs=specs if several else specs[0],
        out_shape=shapes if several else shapes[0],
        scratch_shapes=scratch,
        compiler_params=pltpu.CompilerParams(vmem_limit_bytes=VMEM),
    )


send = call(
    send_kernel,
    "aa",
    "v",
    [((NP * SENT, BS), FLOAT)],
    [pltpu.SMEM((SLOTS, ROWS), jnp.int32), floats(*DIAG), sems(2)],
)
CHUNKS = 4
SELECTED = (NP, WANT, Q, BS)
numbers = [pltpu.SMEM((NP * TILES,), jnp.int32), sems(1 + CHUNKS)]
to_vmem = functools.partial(select_kernel, 0)
to_hbm = functools.partial(select_kernel, CHUNKS)
select = call(to_vmem, "asv", "v", [(SELECTED, FLOAT)], numbers)
select_first = call(to_hbm, "asv", "a", [(SELECTED, FLOAT)], [floats(*SELECTED)] + numbers)
blocks = [floats(WANT * Q * PITCH, BS)]
xs_out = [((2, TILES, BS, BS), HALF), ((2, OWN, BS, BS), HALF)]
held_out = [((OWN, WIDE, BS, BS), FLOAT)]
half_out = [((OWN, SLOTS, BS, BS), FLOAT)] * 2
diag_out = [(DIAG, FLOAT)]
sums_out = [((NP * OWN * Q, BS), FLOAT)]
middle, final = (functools.partial(sweep_kernel, last) for last in (False, True))
first_call = call(first_kernel, "svvvv", "vvvv", xs_out + held_out + sums_out, blocks)
sweep_call = call(middle, "svvvvv", "vvv", held_out + diag_out + sums_out, blocks)
last_call = call(final, "svvvvv", "vvv", half_out + diag_out, blocks)


def to_mate(value):
    return lax.ppermute(value, "k", [(0, 1), (1, 0)])


def swapped(value):
    flat = value.reshape(NP, -1, BS)
    return lax.all_to_all(flat, PEERS, split_axis=0, concat_axis=0, tiled=True)


def on_device(omega_tiles, omega_diag, samples, pattern):
    core = lax.axis_index("k").astype(jnp.int32)
    at = jnp.stack([core, lax.axis_index("y").astype(jnp.int32)])
    in_pairs = omega_tiles.reshape(OWN, CORE, SLOTS, BS, BS)
    other = to_mate(jnp.where(core == 0, in_pairs[:, 1], in_pairs[:, 0]))
    plane = lax.axis_index("zh").astype(jnp.int32).reshape(1)
    came = swapped(send(pattern.T, samples))
    block = came[:, Q, :TILES].astype(jnp.int32)
    row, member = block // ROWS, block % ROWS
    place = (row % Z) // ZL * NP + (row // Z * ZL + row % ZL) * ROWS + turned(member)
    place = place.reshape(NP * TILES)

    def exchanged(mine, select):
        table = lax.all_gather(mine.reshape(NP * Q, BS), "zh").reshape(TABLE_SHAPE)
        return swapped(select(place, plane, table)).reshape(NP * WANT * Q, BS)

    got = exchanged(came[:, :Q], select_first)
    xj, xi, tiles, sums = first_call(at, got, omega_tiles, other, omega_diag)
    diag = omega_diag
    for sweep in range(ITERS):
        parts = swapped(sums).reshape(GROUPS, CORE, Y, OWN * Q, BS)
        got = exchanged(parts.sum(axis=2), select)
        if sweep < ITERS - 1:
            tiles, diag, sums = sweep_call(at, got, tiles, diag, xj, xi)
        else:
            kept, given, diag = last_call(at, got, tiles, diag, xj, xi)
    taken = to_mate(given)
    even = jnp.where(core == 0, kept, taken)
    odd = jnp.where(core == 0, taken, kept)
    return jnp.stack([even, odd], axis=1).reshape(omega_tiles.shape), diag


def solution(mesh):
    fine = Mesh(mesh.devices.reshape(X, ZH, ZL, Y, CORE), ("x", "zh", "zl", "y", "k"))
    rows = ("x", "zh", "zl")
    in_specs = (
        P(rows, COL, None, None),
        P(rows + COL, None),
        P(rows + COL, None),
        P(rows, COL),
    )
    out_specs = (P(rows, COL, None, None), P(rows + COL, None))
    return jax.shard_map(
        on_device, mesh=fine, in_specs=in_specs, out_specs=out_specs, check_vma=False
    )
```
